512 devices in a mesh: bfly: 16 (over x, z_hi), cols: 32 (over z_lo, y, core).
Axes of the slice: x: 4, y: 8, z: 8 (z_hi: 4, z_lo: 2; z = z_hi * 2 + z_lo), core: 2. Of those that a mesh axis runs over, the one named last changes fastest.
Arguments:
- right_side: bfloat16 [16, 32768, 512], P('bfly', 'cols'), may hold values from -6 to 6
- column_leaf_factors: bfloat16 [16, 32768, 256], P('bfly', 'cols'), may hold values from -0.1875 to 0.1875
- leaf_out: bfloat16 [16, 32768, 256], P('bfly', 'cols'), may hold values from -0.0625 to 0.0625
- transfer: bfloat16 [4, 16, 32, 2, 256, 256], P(None, 'bfly', 'cols'), may hold values from -0.25 to 0.25
Outputs:
- solution: float32 [16, 32768, 512], P('bfly', 'cols')
The draws below stay inside these ranges and needn't reach their ends.
All inputs are finite; a program needn't handle non-finite values.
Results may differ from the reference program's by a relative error of at most 0.03.
Values may be sent and summed in bfloat16 or wider, within the bound.
No kernel may reach another device: no remote copies, remote signals or barrier semaphores. Data moves between devices by JAX's collectives and lax.ppermute only.
A program may use at most 64 MiB of HBM per device.

```python
import jax
import jax.numpy as jnp
from jax import lax

L = 1024
RANK = 256
RHS = 512
ITERS = 2
NODES = 16
BLOCKS = 32
SPAN = 32768
CROSS = 4


def levels(key, shape, split, least, largest):
    def one(axis_at, shards_of):
        heights = jax.random.uniform(jax.random.fold_in(jax.random.fold_in(key, 6), axis_at), (shards_of,), jnp.float32, least / len(split), largest / len(split))
        return jnp.repeat(jnp.exp(heights), shape[axis_at] // shards_of).reshape((-1,) + (1,) * (len(shape) - axis_at - 1))

    factor_of = one(*split[0])
    for cut in split[1:]:
        factor_of = factor_of * one(*cut)
    return factor_of


def normal_values(rng, dims, spread, limit, pieces=(), dtype=jnp.bfloat16):
    entries = jax.random.normal(rng, dims, jnp.float32) * spread
    if len(pieces) > 0:
        entries = levels(rng, dims, pieces, -0.22, 0.18) * entries
    return jnp.clip(entries, min=-limit, max=limit).astype(dtype)


def setup_inputs(seed: int = 0) -> dict:
    keys = jax.random.split(jax.random.key(seed), 5)
    return {
        "right_side": normal_values(keys[0], (NODES, SPAN, RHS), 1.0, 6.0, ((0, 16), (1, 32))),
        "column_leaf_factors": normal_values(keys[1], (NODES, SPAN, RANK), L ** -0.5, 0.1875, ((0, 16), (1, 32))),
        "leaf_out": normal_values(keys[2], (NODES, SPAN, RANK), (RANK * BLOCKS) ** -0.5, 0.0625, ((0, 16), (1, 32))),
        "transfer": normal_values(keys[3], (CROSS, NODES, BLOCKS, 2, RANK, RANK), (2 * RANK) ** -0.5, 0.25, ((1, 16), (2, 32))),
    }


def project_onto_leaves(operands):
    iterate, basis_rows = operands
    input_vector = iterate.astype(jnp.bfloat16).reshape(BLOCKS, L, RHS).astype(jnp.float32)
    leaf_factor_rows = basis_rows.reshape(BLOCKS, L, RANK).astype(jnp.float32)
    return jnp.einsum("aiq,ais->aqs", leaf_factor_rows, input_vector).astype(jnp.bfloat16)


def expand(operands):
    basis_rows, reduced_total = operands
    leaf_factor_rows = basis_rows.reshape(BLOCKS, L, RANK).astype(jnp.float32)
    result_row_values = jnp.einsum("nfw,wp->nfp", leaf_factor_rows, reduced_total.astype(jnp.float32))
    return result_row_values.reshape(SPAN, RHS)


def apply_operator(iterate, column_leaf_factors, leaf_out, transfer):
    coefficient = lax.map(project_onto_leaves, (iterate, column_leaf_factors))
    for level_index in range(CROSS):
        distance = 2 ** level_index
        shaped = coefficient.reshape(NODES // (2 * distance), 2, distance, BLOCKS, RANK, RHS)
        partner = jnp.flip(shaped, axis=1).reshape(NODES, BLOCKS, RANK, RHS)
        operator_blocks = transfer[level_index].astype(jnp.float32)
        combined = jnp.einsum("pcij,pcjr->pcir", operator_blocks[:, :, 0], coefficient.astype(jnp.float32))
        combined = combined + jnp.einsum("pcij,pcjr->pcir", operator_blocks[:, :, 1], partner.astype(jnp.float32))
        coefficient = combined.astype(jnp.bfloat16)
    reduced_total = jnp.sum(coefficient.astype(jnp.float32), axis=1).astype(jnp.bfloat16)
    return lax.map(expand, (leaf_out, reduced_total))


def reference(right_side, column_leaf_factors, leaf_out, transfer):
    initial = right_side.astype(jnp.float32)
    iterate = initial
    for iteration in range(ITERS):
        iterate = initial - apply_operator(iterate, column_leaf_factors, leaf_out, transfer)
    return iterate
```

```python
import jax
import jax.numpy as jnp
from jax import lax
from jax.experimental import pallas as pl
from jax.experimental.pallas import tpu as pltpu
from jax.sharding import Mesh, PartitionSpec as P

ITERS = 2
BF = jnp.bfloat16
F32 = jnp.float32
LINE = ("zl", "y")


def swap(block, axis, bit):
    size = lax.axis_size(axis)
    return lax.ppermute(block, axis, [(i, i ^ bit) for i in range(size)])


def mm(spec, a, b):
    return jnp.einsum(spec, a, b, preferred_element_type=F32)


def by_target(blocks):
    me = lax.axis_index("x")
    for bit in (1, 2):
        turned = [blocks[d ^ bit] for d in range(len(blocks))]
        blocks = [jnp.where(me & bit == bit, t, b) for t, b in zip(turned, blocks)]
    return blocks


def finish_kernel(rhs_ref, basis_ref, total_ref, out_ref):
    half = total_ref.shape[2]
    for core in range(2):
        cols = slice(core * half, (core + 1) * half)
        update = jnp.dot(basis_ref[...], total_ref[core], preferred_element_type=F32)
        out_ref[:, cols] = rhs_ref[:, cols].astype(F32) - update


def finish(rhs, basis, total):
    rows, width = rhs.shape
    rank = basis.shape[1]
    block = rows // 4
    return pl.pallas_call(
        finish_kernel,
        grid=(rows // block,),
        in_specs=[
            pl.BlockSpec((block, width), lambda i: (i, 0)),
            pl.BlockSpec((block, rank), lambda i: (i, 0)),
            pl.BlockSpec(total.shape, lambda i: (0, 0, 0)),
        ],
        out_specs=pl.BlockSpec((block, width), lambda i: (i, 0)),
        out_shape=jax.ShapeDtypeStruct((rows, width), F32),
    )(rhs, basis, total)


def body(right_side, column_leaf_factors, leaf_out, transfer):
    rhs = right_side[0]
    basis = column_leaf_factors[0]
    out_basis = leaf_out[0]
    half = rhs.shape[1] // 2
    rank = basis.shape[1]
    core = lax.axis_index("c")

    first = mm("lk,lr->kr", basis, rhs).astype(BF)
    first = lax.all_gather(first, "c")
    first = lax.dynamic_slice_in_dim(first, core * half, half, 2)
    first, transfer, basis_late = lax.optimization_barrier((first, transfer, basis))

    own = transfer[:, 0, 0, 0]
    other = transfer[:, 0, 0, 1]
    far = swap(other[3], "x", 2)
    levels = [lax.all_gather(transfer[0, 0, 0], "c")]
    gram = mm("li,lj->ij", basis_late, out_basis).astype(BF)
    more = lax.all_gather(jnp.concatenate([transfer[1, 0, 0], gram[None]], 0), "c")
    levels.append(more[:, :2])
    gram = more[:, 2]
    wide = jnp.concatenate([own[3], far], 0)
    kept = mm("ij,jk->ik", wide, own[2]).astype(BF)
    sent = mm("ij,jk->ik", wide, other[2]).astype(BF)
    came = swap(sent, "x", 1)
    tail = by_target([kept[:rank], came[:rank], kept[rank:], came[rank:]])
    tail = [lax.all_gather(jnp.concatenate(tail[i : i + 2], 0), "c") for i in (0, 2)]

    coefficient = first
    for iteration in range(ITERS):
        for level, axis in enumerate(("za", "zb")):
            partner = swap(coefficient, axis, 1)
            coefficient = (
                mm("cij,cjr->cir", levels[level][:, 0], coefficient)
                + mm("cij,cjr->cir", levels[level][:, 1], partner)
            ).astype(BF)
        spread = jnp.concatenate([mm("cij,cjr->ir", t, coefficient).astype(BF) for t in tail], 0)
        count = lax.axis_size(("x",) + LINE)
        pieces = spread.reshape(count, -1, half)
        pieces = lax.all_to_all(pieces, ("x",) + LINE, 0, 0, tiled=True)
        share = jnp.sum(pieces.astype(F32), axis=0).astype(BF)
        copies = jnp.broadcast_to(share, (lax.axis_size(LINE), *share.shape))
        total = lax.all_to_all(copies, LINE, 0, 0, tiled=True).reshape(rank, half)
        if iteration < ITERS - 1:
            coefficient = (first.astype(F32) - mm("cij,jr->cir", gram, total)).astype(BF)
    total = lax.all_gather(total, "c")
    return finish(rhs, out_basis, total)[None]


def solution(mesh):
    devices = mesh.devices.reshape(4, 2, 2, 2, 8, 2)
    fine = Mesh(devices, ("x", "zb", "za", "zl", "y", "c"))
    bfly, cols = ("x", "zb", "za"), ("zl", "y", "c")
    in_specs = (
        P(bfly, cols, None),
        P(bfly, cols, None),
        P(bfly, cols, None),
        P(None, bfly, cols, None, None, None),
    )
    out_specs = P(bfly, cols, None)
    return jax.shard_map(body, mesh=fine, in_specs=in_specs, out_specs=out_specs, check_vma=False)
```

```python
import jax
import jax.numpy as jnp
from jax import lax
from jax.experimental import pallas as pl
from jax.experimental.pallas import tpu as pltpu
from jax.sharding import Mesh, PartitionSpec as P

ITERS = 2
PARTS = 2
BF = jnp.bfloat16
F32 = jnp.float32
LINE = ("zl", "y")


def swap(block, axis, bit):
    size = lax.axis_size(axis)
    return lax.ppermute(block, axis, [(i, i ^ bit) for i in range(size)])


def mm(spec, a, b):
    return jnp.einsum(spec, a, b, preferred_element_type=F32)


def by_target(blocks):
    me = lax.axis_index("x")
    for bit in (1, 2):
        turned = [blocks[d ^ bit] for d in range(len(blocks))]
        blocks = [jnp.where(me & bit == bit, t, b) for t, b in zip(turned, blocks)]
    return blocks


def mix(pair, mine, partner):
    return (mm("cij,cjr->cir", pair[:, 0], mine) + mm("cij,cjr->cir", pair[:, 1], partner)).astype(BF)


def add_up(tail, coefficient):
    spread = jnp.concatenate([mm("cij,cjr->ir", t, coefficient).astype(BF) for t in tail], 0)
    count = lax.axis_size(("x",) + LINE)
    pieces = spread.reshape(count, -1, coefficient.shape[2])
    pieces = lax.all_to_all(pieces, ("x",) + LINE, 0, 0, tiled=True)
    return jnp.sum(pieces.astype(F32), axis=0).astype(BF)


def hand_out(share, rank):
    copies = jnp.broadcast_to(share, (lax.axis_size(LINE), *share.shape))
    return lax.all_to_all(copies, LINE, 0, 0, tiled=True).reshape(rank, -1)


def finish_kernel(rhs_ref, basis_ref, total_ref, out_ref):
    half = total_ref.shape[2]
    for core in range(2):
        cols = slice(core * half, (core + 1) * half)
        update = jnp.dot(basis_ref[...], total_ref[core], preferred_element_type=F32)
        out_ref[:, cols] = rhs_ref[:, cols].astype(F32) - update


def finish(rhs, basis, total):
    rows, width = rhs.shape
    rank = basis.shape[1]
    block = rows // 4
    return pl.pallas_call(
        finish_kernel,
        grid=(rows // block,),
        in_specs=[
            pl.BlockSpec((block, width), lambda i: (i, 0)),
            pl.BlockSpec((block, rank), lambda i: (i, 0)),
            pl.BlockSpec(total.shape, lambda i: (0, 0, 0)),
        ],
        out_specs=pl.BlockSpec((block, width), lambda i: (i, 0)),
        out_shape=jax.ShapeDtypeStruct((rows, width), F32),
    )(rhs, basis, total)


def body(right_side, column_leaf_factors, leaf_out, transfer):
    rhs = right_side[0]
    basis = column_leaf_factors[0]
    out_basis = leaf_out[0]
    half = rhs.shape[1] // 2
    part = half // PARTS
    rank = basis.shape[1]
    core = lax.axis_index("c")

    first = mm("lk,lr->kr", basis, rhs).astype(BF)
    first = lax.all_gather(first, "c")
    first = lax.dynamic_slice_in_dim(first, core * half, half, 2)
    first, transfer, basis_late = lax.optimization_barrier((first, transfer, basis))

    own = transfer[:, 0, 0, 0]
    other = transfer[:, 0, 0, 1]
    far = swap(other[3], "x", 2)
    levels = [lax.all_gather(transfer[0, 0, 0], "c")]
    gram = mm("li,lj->ij", basis_late, out_basis).astype(BF)
    more = lax.all_gather(jnp.concatenate([transfer[1, 0, 0], gram[None]], 0), "c")
    levels.append(more[:, :2])
    gram = more[:, 2]
    wide = jnp.concatenate([own[3], far], 0)
    kept = mm("ij,jk->ik", wide, own[2]).astype(BF)
    sent = mm("ij,jk->ik", wide, other[2]).astype(BF)
    came = swap(sent, "x", 1)
    tail = by_target([kept[:rank], came[:rank], kept[rank:], came[rank:]])
    tail = [lax.all_gather(jnp.concatenate(tail[i : i + 2], 0), "c") for i in (0, 2)]

    parts = [first[:, :, i * part : (i + 1) * part] for i in range(PARTS)]
    coefficients = list(parts)
    for iteration in range(ITERS):
        for level, axis in enumerate(("za", "zb")):
            for i in range(PARTS):
                coefficients[i] = mix(levels[level], coefficients[i], swap(coefficients[i], axis, 1))
        shares = [None] * PARTS
        for i in range(PARTS):
            shares[i] = add_up(tail, coefficients[i])
        totals = [hand_out(share, rank) for share in shares]
        if iteration < ITERS - 1:
            for i in range(PARTS):
                coefficients[i] = (parts[i].astype(F32) - mm("cij,jr->cir", gram, totals[i])).astype(BF)
    total = jnp.concatenate(totals, 1)
    total = lax.all_gather(total, "c")
    return finish(rhs, out_basis, total)[None]


def solution(mesh):
    devices = mesh.devices.reshape(4, 2, 2, 2, 8, 2)
    fine = Mesh(devices, ("x", "zb", "za", "zl", "y", "c"))
    bfly, cols = ("x", "zb", "za"), ("zl", "y", "c")
    in_specs = (
        P(bfly, cols, None),
        P(bfly, cols, None),
        P(bfly, cols, None),
        P(None, bfly, cols, None, None, None),
    )
    out_specs = P(bfly, cols, None)
    return jax.shard_map(body, mesh=fine, in_specs=in_specs, out_specs=out_specs, check_vma=False)
```

```python
import jax
import jax.numpy as jnp
from jax import lax
from jax.experimental import pallas as pl
from jax.experimental.pallas import tpu as pltpu
from jax.sharding import Mesh, PartitionSpec as P

BF = jnp.bfloat16
F32 = jnp.float32
LINE = ("zl", "y")
QUAD = ("zb", "za")
CHUNKS = 4


def swap(block, axis, bit):
    size = lax.axis_size(axis)
    return lax.ppermute(block, axis, [(i, i ^ bit) for i in range(size)])


def mm(spec, a, b):
    return jnp.einsum(spec, a, b, preferred_element_type=F32)


def dot(a, b):
    return jnp.dot(a, b, preferred_element_type=F32)


def in_order(blocks, axis):
    me = lax.axis_index(axis)
    for bit in (1, 2):
        turned = [blocks[d ^ bit] for d in range(len(blocks))]
        blocks = [jnp.where(me & bit == bit, t, b) for t, b in zip(turned, blocks)]
    return blocks


def add_up(tail, coefficient):
    spread = jnp.concatenate([mm("cij,cjr->ir", t, coefficient).astype(BF) for t in tail], 0)
    group = ("x",) + LINE
    pieces = spread.reshape(lax.axis_size(group), -1, coefficient.shape[2])
    pieces = lax.all_to_all(pieces, group, 0, 0, tiled=True)
    return jnp.sum(pieces.astype(F32), axis=0).astype(BF)


def hand_out(share, axes):
    copies = jnp.broadcast_to(share, (lax.axis_size(axes), *share.shape))
    return lax.all_to_all(copies, axes, 0, 0, tiled=True)


def finish_kernel(rhs_hbm, basis_hbm, total_hbm, out_hbm, rhs, basis, total, out, sems):
    rows = rhs.shape[0] // CHUNKS
    half = total.shape[2]
    first = pltpu.make_async_copy(total_hbm, total, sems.at[0, CHUNKS])
    first.start()
    loads = []
    for i in range(CHUNKS):
        part = pl.ds(i * rows, rows)
        loads.append(
            (
                pltpu.make_async_copy(basis_hbm.at[part], basis.at[part], sems.at[0, i]),
                pltpu.make_async_copy(rhs_hbm.at[part], rhs.at[part], sems.at[1, i]),
            )
        )
        for load in loads[-1]:
            load.start()
    first.wait()
    stores = []
    for i in range(CHUNKS):
        part = pl.ds(i * rows, rows)
        for load in loads[i]:
            load.wait()
        for core in range(2):
            cols = slice(core * half, (core + 1) * half)
            out[part, cols] = rhs[part, cols].astype(F32) - dot(basis[part], total[core])
        stores.append(pltpu.make_async_copy(out.at[part], out_hbm.at[part], sems.at[2, i]))
        stores[-1].start()
    for store in stores:
        store.wait()


def finish(rhs, basis, total):
    return pl.pallas_call(
        finish_kernel,
        in_specs=[pl.BlockSpec(memory_space=pl.ANY)] * 3,
        out_specs=pl.BlockSpec(memory_space=pl.ANY),
        out_shape=jax.ShapeDtypeStruct(rhs.shape, F32),
        scratch_shapes=[
            pltpu.VMEM(rhs.shape, BF),
            pltpu.VMEM(basis.shape, BF),
            pltpu.VMEM(total.shape, BF),
            pltpu.VMEM(rhs.shape, F32),
            pltpu.SemaphoreType.DMA((3, CHUNKS + 1)),
        ],
        compiler_params=pltpu.CompilerParams(vmem_limit_bytes=16 * 1024 * 1024),
    )(rhs, basis, total)


def body(right_side, column_leaf_factors, leaf_out, transfer):
    rhs, basis, out_basis = right_side[0], column_leaf_factors[0], leaf_out[0]
    half = rhs.shape[1] // 2
    rank = basis.shape[1]
    core = lax.axis_index("c")

    start = mm("lk,lr->kr", basis, rhs).astype(BF)
    start, transfer, basis, out_late = lax.optimization_barrier((start, transfer, basis, out_basis))
    own = transfer[:, 0, 0, 0]
    other = transfer[:, 0, 0, 1]
    gram = mm("li,lj->ij", basis, out_late).astype(BF)
    gram, far = lax.optimization_barrier((gram, other[3]))
    far = swap(far, "x", 2)

    field = (dot(own[0], start) + dot(other[0], swap(start, "za", 1))).astype(BF)
    near = swap(gram, "za", 1)
    field, near = lax.optimization_barrier((field, near))
    chain = jnp.concatenate([dot(own[0], gram).astype(BF), dot(other[0], near).astype(BF)], 1)
    field = (dot(own[1], field) + dot(other[1], swap(field, "zb", 1))).astype(BF)

    wide = jnp.concatenate([own[3], far], 0)
    kept = dot(wide, own[2]).astype(BF)
    came = swap(dot(wide, other[2]).astype(BF), "x", 1)
    tail = in_order([kept[:rank], came[:rank], kept[rank:], came[rank:]], "x")
    tail = [lax.all_gather(jnp.concatenate(tail[i : i + 2], 0), "c") for i in (0, 2)]

    field = lax.all_gather(field, "c")
    field = lax.dynamic_slice_in_dim(field, core * half, half, 2)
    share = add_up(tail, field)
    totals = hand_out(share, QUAD + LINE).reshape(2, 2 * rank, half)

    chain_far = swap(chain, "zb", 1)
    mine = dot(own[1], chain).astype(BF)
    theirs = dot(other[1], chain_far).astype(BF)
    back = in_order([mine[:, :rank], mine[:, rank:], theirs[:, :rank], theirs[:, rank:]], QUAD)
    back = [lax.all_gather(jnp.concatenate(back[i : i + 2], 1), "c") for i in (0, 2)]

    change = mm("cij,jr->cir", back[0], totals[0]) + mm("cij,jr->cir", back[1], totals[1])
    field = (field.astype(F32) - change).astype(BF)
    share = add_up(tail, field)
    total = hand_out(share, LINE).reshape(rank, half)
    return finish(rhs, out_basis, lax.all_gather(total, "c"))[None]


def solution(mesh):
    devices = mesh.devices.reshape(4, 2, 2, 2, 8, 2)
    fine = Mesh(devices, ("x", "zb", "za", "zl", "y", "c"))
    bfly, cols = ("x", "zb", "za"), ("zl", "y", "c")
    in_specs = (
        P(bfly, cols, None),
        P(bfly, cols, None),
        P(bfly, cols, None),
        P(None, bfly, cols, None, None, None),
    )
    out_specs = P(bfly, cols, None)
    return jax.shard_map(body, mesh=fine, in_specs=in_specs, out_specs=out_specs, check_vma=False)
```

```python
import jax
import jax.numpy as jnp
from jax import lax
from jax.experimental import pallas as pl
from jax.experimental.pallas import tpu as pltpu
from jax.sharding import Mesh, PartitionSpec as P

BF = jnp.bfloat16
F32 = jnp.float32
LINE = ("y", "zl")
GROUP = LINE + ("x",)
QUAD = ("zb", "za")
CHUNKS = 4


def swap(block, axis, bit):
    size = lax.axis_size(axis)
    return lax.ppermute(block, axis, [(i, i ^ bit) for i in range(size)])


def mm(spec, a, b):
    return jnp.einsum(spec, a, b, preferred_element_type=F32)


def dot(a, b):
    return jnp.dot(a, b, preferred_element_type=F32)


def in_order(blocks, axis):
    me = lax.axis_index(axis)
    for bit in (1, 2):
        turned = [blocks[d ^ bit] for d in range(len(blocks))]
        blocks = [jnp.where(me & bit == bit, t, b) for t, b in zip(turned, blocks)]
    return blocks


def add_up(tail, coefficient):
    spread = mm("cij,cjr->ir", tail, coefficient).astype(BF)
    pieces = spread.reshape(lax.axis_size(GROUP), -1, coefficient.shape[2])
    pieces = lax.all_to_all(pieces, GROUP, 0, 0, tiled=True)
    return jnp.sum(pieces.astype(F32), axis=0).astype(BF)


def hand_out(share, axes):
    copies = jnp.broadcast_to(share, (lax.axis_size(axes), *share.shape))
    return lax.all_to_all(copies, axes, 0, 0, tiled=True)


def finish_kernel(rhs_hbm, basis_hbm, total_hbm, out_hbm, rhs, basis, total, out, sems):
    rows = rhs.shape[0] // CHUNKS
    half = total.shape[2]
    first = pltpu.make_async_copy(total_hbm, total, sems.at[0, CHUNKS])
    first.start()
    loads = []
    for i in range(CHUNKS):
        part = pl.ds(i * rows, rows)
        loads.append(
            (
                pltpu.make_async_copy(basis_hbm.at[part], basis.at[part], sems.at[0, i]),
                pltpu.make_async_copy(rhs_hbm.at[part], rhs.at[part], sems.at[1, i]),
            )
        )
        for load in loads[-1]:
            load.start()
    first.wait()
    stores = []
    for i in range(CHUNKS):
        part = pl.ds(i * rows, rows)
        for load in loads[i]:
            load.wait()
        for core in range(2):
            cols = slice(core * half, (core + 1) * half)
            out[part, cols] = rhs[part, cols].astype(F32) - dot(basis[part], total[core])
        stores.append(pltpu.make_async_copy(out.at[part], out_hbm.at[part], sems.at[2, i]))
        stores[-1].start()
    for store in stores:
        store.wait()


def finish(rhs, basis, total):
    return pl.pallas_call(
        finish_kernel,
        in_specs=[pl.BlockSpec(memory_space=pl.ANY)] * 3,
        out_specs=pl.BlockSpec(memory_space=pl.ANY),
        out_shape=jax.ShapeDtypeStruct(rhs.shape, F32),
        scratch_shapes=[
            pltpu.VMEM(rhs.shape, BF),
            pltpu.VMEM(basis.shape, BF),
            pltpu.VMEM(total.shape, BF),
            pltpu.VMEM(rhs.shape, F32),
            pltpu.SemaphoreType.DMA((3, CHUNKS + 1)),
        ],
        compiler_params=pltpu.CompilerParams(vmem_limit_bytes=16 * 1024 * 1024),
    )(rhs, basis, total)


def body(right_side, column_leaf_factors, leaf_out, transfer):
    rhs, basis, out_basis = right_side[0], column_leaf_factors[0], leaf_out[0]
    half = rhs.shape[1] // 2
    rank = basis.shape[1]
    core = lax.axis_index("c")

    start = mm("lk,lr->kr", basis, rhs).astype(BF)
    start, transfer = lax.optimization_barrier((start, transfer))
    own = transfer[:, 0, 0, 0]
    other = transfer[:, 0, 0, 1]

    kept_part = dot(own[0], start)
    kept_part, far = lax.optimization_barrier((kept_part, other[3]))
    far = swap(far, "x", 2)
    field = (kept_part + dot(other[0], swap(start, "za", 1))).astype(BF)
    field = (dot(own[1], field) + dot(other[1], swap(field, "zb", 1))).astype(BF)

    wide = jnp.concatenate([own[3], far], 0)
    kept = dot(wide, own[2]).astype(BF)
    came = swap(dot(wide, other[2]).astype(BF), "x", 1)
    tail = in_order([kept[:rank], came[:rank], kept[rank:], came[rank:]], "x")
    tail = jnp.stack([t.reshape(lax.axis_size(LINE), -1, rank) for t in tail], 1).reshape(4 * rank, rank)
    tail = [lax.all_gather(tail[i : i + 2 * rank], "c") for i in (0, 2 * rank)]
    tail = jnp.concatenate(tail, 1)

    tail, basis = lax.optimization_barrier((tail, basis))
    gram = mm("li,lj->ij", basis, out_basis).astype(BF)
    near = swap(gram, "za", 1)

    field = lax.all_gather(field, "c")
    field, near = lax.optimization_barrier((field, near))
    chain = jnp.concatenate([dot(own[0], gram).astype(BF), dot(other[0], near).astype(BF)], 1)
    field = lax.dynamic_slice_in_dim(field, core * half, half, 2)
    share = add_up(tail, field)
    totals = hand_out(share, QUAD + LINE).reshape(4 * rank, half)

    chain_far = swap(chain, "zb", 1)
    mine = dot(own[1], chain).astype(BF)
    theirs = dot(other[1], chain_far).astype(BF)
    back = in_order([mine[:, :rank], mine[:, rank:], theirs[:, :rank], theirs[:, rank:]], QUAD)
    back = [lax.all_gather(jnp.concatenate(back[i : i + 2], 1), "c") for i in (0, 2)]
    back = jnp.concatenate(back, 2)

    field = (field.astype(F32) - mm("cij,jr->cir", back, totals)).astype(BF)
    share = add_up(tail, lax.optimization_barrier(field))
    total = hand_out(share, LINE).reshape(rank, half)
    return finish(rhs, out_basis, lax.all_gather(total, "c"))[None]


def solution(mesh):
    devices = mesh.devices.reshape(4, 2, 2, 2, 8, 2)
    fine = Mesh(devices, ("x", "zb", "za", "zl", "y", "c"))
    bfly, cols = ("x", "zb", "za"), ("zl", "y", "c")
    in_specs = (
        P(bfly, cols, None),
        P(bfly, cols, None),
        P(bfly, cols, None),
        P(None, bfly, cols, None, None, None),
    )
    out_specs = P(bfly, cols, None)
    return jax.shard_map(body, mesh=fine, in_specs=in_specs, out_specs=out_specs, check_vma=False)
```

```python
import jax
import jax.numpy as jnp
from jax import lax
from jax.experimental import pallas as pl
from jax.experimental.pallas import tpu as pltpu
from jax.experimental.layout import Layout, with_layout_constraint
from jax.sharding import Mesh, PartitionSpec as P

BF = jnp.bfloat16
F32 = jnp.float32
LINE = ("y", "zl")
GROUP = LINE + ("x",)
QUAD = ("zb", "za")
CHUNKS = 4


def swap(block, axis, bit):
    size = lax.axis_size(axis)
    return lax.ppermute(block, axis, [(i, i ^ bit) for i in range(size)])


def mm(spec, a, b):
    return jnp.einsum(spec, a, b, preferred_element_type=F32)


def dot(a, b):
    return jnp.dot(a, b, preferred_element_type=F32)


def in_rows(block):
    return with_layout_constraint(block, Layout(major_to_minor=(0, 1)))


def in_order(blocks, axis):
    me = lax.axis_index(axis)
    for bit in (1, 2):
        turned = [blocks[d ^ bit] for d in range(len(blocks))]
        blocks = [jnp.where(me & bit == bit, t, b) for t, b in zip(turned, blocks)]
    return blocks


def add_up(tail, coefficient):
    spread = mm("cij,cjr->ir", tail, coefficient).astype(BF)
    pieces = spread.reshape(lax.axis_size(GROUP), -1, coefficient.shape[2])
    pieces = lax.all_to_all(pieces, GROUP, 0, 0, tiled=True)
    return jnp.sum(pieces.astype(F32), axis=0).astype(BF)


def hand_out(share, axes):
    copies = jnp.broadcast_to(share, (lax.axis_size(axes), *share.shape))
    return lax.all_to_all(copies, axes, 0, 0, tiled=True)


def finish_kernel(rhs_hbm, basis_hbm, total_hbm, out_hbm, rhs, basis, total, out, sems):
    rows = rhs.shape[0] // CHUNKS
    half = total.shape[2]
    first = pltpu.make_async_copy(total_hbm, total, sems.at[0, CHUNKS])
    first.start()
    loads = []
    for i in range(CHUNKS):
        part = pl.ds(i * rows, rows)
        loads.append(
            (
                pltpu.make_async_copy(basis_hbm.at[part], basis.at[part], sems.at[0, i]),
                pltpu.make_async_copy(rhs_hbm.at[part], rhs.at[part], sems.at[1, i]),
            )
        )
        for load in loads[-1]:
            load.start()
    first.wait()
    stores = []
    for i in range(CHUNKS):
        part = pl.ds(i * rows, rows)
        for load in loads[i]:
            load.wait()
        for core in range(2):
            cols = slice(core * half, (core + 1) * half)
            out[part, cols] = rhs[part, cols].astype(F32) - dot(basis[part], total[core])
        stores.append(pltpu.make_async_copy(out.at[part], out_hbm.at[part], sems.at[2, i]))
        stores[-1].start()
    for store in stores:
        store.wait()


def finish(rhs, basis, total):
    return pl.pallas_call(
        finish_kernel,
        in_specs=[pl.BlockSpec(memory_space=pl.ANY)] * 3,
        out_specs=pl.BlockSpec(memory_space=pl.ANY),
        out_shape=jax.ShapeDtypeStruct(rhs.shape, F32),
        scratch_shapes=[
            pltpu.VMEM(rhs.shape, BF),
            pltpu.VMEM(basis.shape, BF),
            pltpu.VMEM(total.shape, BF),
            pltpu.VMEM(rhs.shape, F32),
            pltpu.SemaphoreType.DMA((3, CHUNKS + 1)),
        ],
        compiler_params=pltpu.CompilerParams(vmem_limit_bytes=16 * 1024 * 1024),
    )(rhs, basis, total)


def body(right_side, column_leaf_factors, leaf_out, transfer):
    rhs, basis, out_basis = right_side[0], column_leaf_factors[0], leaf_out[0]
    half = rhs.shape[1] // 2
    rank = basis.shape[1]
    core = lax.axis_index("c")

    tie = lax.optimization_barrier
    start = mm("lk,lr->kr", basis, rhs).astype(BF)
    start, transfer, basis = tie((start, transfer, basis))
    own = transfer[:, 0, 0, 0]
    other = transfer[:, 0, 0, 1]

    far = swap(other[3], "x", 2)
    field = (dot(own[0], start) + dot(other[0], swap(start, "za", 1))).astype(BF)
    field, far = tie((field, far))

    wide = jnp.concatenate([own[3], far], 0)
    sent = dot(wide, other[2]).astype(BF)
    came = swap(sent, "x", 1)
    field = (dot(own[1], field) + dot(other[1], swap(field, "zb", 1))).astype(BF)
    field, came, basis, wide = tie((field, came, basis, wide))
    middle = field

    gram = mm("li,lj->ij", basis, out_basis).astype(BF)
    near = swap(gram, "za", 1)
    field = (dot(own[2], field) + dot(other[2], swap(field, "x", 1))).astype(BF)
    field, gram_late, near = tie((field, gram, near))

    chain = [dot(own[0], gram_late).astype(BF), dot(other[0], near).astype(BF)]
    chain_far = [swap(chain[0], "zb", 1), None]
    field = (dot(own[3], field) + dot(other[3], swap(field, "x", 2))).astype(BF)
    both = lax.all_gather(field, "c")
    both = lax.dynamic_slice_in_dim(both, core * half, half, 2)
    both = (both[0].astype(F32) + both[1].astype(F32)).astype(BF)
    both, chain[1], middle = tie((both, chain[1], middle))
    chain_far[1] = swap(chain[1], "zb", 1)
    middle = lax.all_gather(middle, "c")
    middle = lax.dynamic_slice_in_dim(middle, core * half, half, 2)
    pieces = lax.all_to_all(both.reshape(lax.axis_size(LINE), -1, half), LINE, 0, 0, tiled=True)
    share = jnp.sum(pieces.astype(F32), axis=0).astype(BF)
    share, *chain_far, came, wide = tie((share, *chain_far, came, wide))
    totals = hand_out(share, QUAD + LINE).reshape(4 * rank, half)

    kept = dot(wide, own[2]).astype(BF)
    tail = in_order([kept[:rank], came[:rank], kept[rank:], came[rank:]], "x")
    tail = jnp.stack([t.reshape(lax.axis_size(LINE), -1, rank) for t in tail], 1).reshape(4 * rank, rank)
    tail = [lax.all_gather(tail[i : i + 2 * rank], "c") for i in (0, 2 * rank)]
    tail = jnp.concatenate(tail, 1)

    back = [dot(own[1], c).astype(BF) for c in chain] + [dot(other[1], c).astype(BF) for c in chain_far]
    back = in_order(back, QUAD)
    back = [in_rows(jnp.concatenate(back[i : i + 2], 1)) for i in (0, 2)]
    back = [lax.all_gather(b, "c") for b in back]
    back = jnp.concatenate(back, 2)

    middle, tail, back, totals = tie((middle, tail, back, totals))
    field = tie((middle.astype(F32) - mm("cij,jr->cir", back, totals)).astype(BF))
    share = add_up(tail, field)
    total = hand_out(share, LINE).reshape(rank, half)
    return finish(rhs, out_basis, lax.all_gather(total, "c"))[None]


def solution(mesh):
    devices = mesh.devices.reshape(4, 2, 2, 2, 8, 2)
    fine = Mesh(devices, ("x", "zb", "za", "zl", "y", "c"))
    bfly, cols = ("x", "zb", "za"), ("zl", "y", "c")
    in_specs = (
        P(bfly, cols, None),
        P(bfly, cols, None),
        P(bfly, cols, None),
        P(None, bfly, cols, None, None, None),
    )
    out_specs = P(bfly, cols, None)
    return jax.shard_map(body, mesh=fine, in_specs=in_specs, out_specs=out_specs, check_vma=False)
```

```python
import jax
import jax.numpy as jnp
from jax import lax
from jax.experimental import pallas as pl
from jax.experimental.pallas import tpu as pltpu
from jax.sharding import Mesh, PartitionSpec as P

BF = jnp.bfloat16
F32 = jnp.float32
LINE = ("zl", "y")
GROUP = ("x",) + LINE
QUAD = ("zb", "za")
CHUNKS = 4


def swap(block, axis, bit):
    size = lax.axis_size(axis)
    return lax.ppermute(block, axis, [(i, i ^ bit) for i in range(size)])


def mm(spec, a, b):
    return jnp.einsum(spec, a, b, preferred_element_type=F32)


def dot(a, b):
    return jnp.dot(a, b, preferred_element_type=F32)


def in_order(blocks, axis):
    me = lax.axis_index(axis)
    for bit in (1, 2):
        turned = [blocks[d ^ bit] for d in range(len(blocks))]
        blocks = [jnp.where(me & bit == bit, t, b) for t, b in zip(turned, blocks)]
    return blocks


def add_up(tail, coefficient):
    spread = mm("cij,cjr->ir", tail, coefficient).astype(BF)
    pieces = spread.reshape(lax.axis_size(GROUP), -1, coefficient.shape[2])
    pieces = lax.all_to_all(pieces, GROUP, 0, 0, tiled=True)
    return jnp.sum(pieces.astype(F32), axis=0).astype(BF)


def hand_out(share, axes):
    copies = jnp.broadcast_to(share, (lax.axis_size(axes), *share.shape))
    return lax.all_to_all(copies, axes, 0, 0, tiled=True)


def finish_kernel(rhs_hbm, basis_hbm, total_hbm, out_hbm, rhs, basis, total, out, sems):
    rows = rhs.shape[0] // CHUNKS
    half = total.shape[2]
    first = pltpu.make_async_copy(total_hbm, total, sems.at[0, CHUNKS])
    first.start()
    loads = []
    for i in range(CHUNKS):
        part = pl.ds(i * rows, rows)
        loads.append(
            (
                pltpu.make_async_copy(basis_hbm.at[part], basis.at[part], sems.at[0, i]),
                pltpu.make_async_copy(rhs_hbm.at[part], rhs.at[part], sems.at[1, i]),
            )
        )
        for load in loads[-1]:
            load.start()
    first.wait()
    stores = []
    for i in range(CHUNKS):
        part = pl.ds(i * rows, rows)
        for load in loads[i]:
            load.wait()
        for core in range(2):
            cols = slice(core * half, (core + 1) * half)
            out[part, cols] = rhs[part, cols].astype(F32) - dot(basis[part], total[core])
        stores.append(pltpu.make_async_copy(out.at[part], out_hbm.at[part], sems.at[2, i]))
        stores[-1].start()
    for store in stores:
        store.wait()


def finish(rhs, basis, total):
    return pl.pallas_call(
        finish_kernel,
        in_specs=[pl.BlockSpec(memory_space=pl.ANY)] * 3,
        out_specs=pl.BlockSpec(memory_space=pl.ANY),
        out_shape=jax.ShapeDtypeStruct(rhs.shape, F32),
        scratch_shapes=[
            pltpu.VMEM(rhs.shape, BF),
            pltpu.VMEM(basis.shape, BF),
            pltpu.VMEM(total.shape, BF),
            pltpu.VMEM(rhs.shape, F32),
            pltpu.SemaphoreType.DMA((3, CHUNKS + 1)),
        ],
        compiler_params=pltpu.CompilerParams(vmem_limit_bytes=16 * 1024 * 1024),
    )(rhs, basis, total)


def body(right_side, column_leaf_factors, leaf_out, transfer):
    rhs, basis, out_basis = right_side[0], column_leaf_factors[0], leaf_out[0]
    half = rhs.shape[1] // 2
    rank = basis.shape[1]
    core = lax.axis_index("c")

    tie = lax.optimization_barrier
    start = mm("lk,lr->kr", basis, rhs).astype(BF)
    start, transfer = tie((start, transfer))
    own = transfer[:, 0, 0, 0]
    other = transfer[:, 0, 0, 1]

    far = swap(other[3], "x", 2)
    field = (dot(own[0], start) + dot(other[0], swap(start, "za", 1))).astype(BF)
    field, far = tie((field, far))
    wide = jnp.concatenate([own[3], far], 0)
    came = swap(dot(wide, other[2]).astype(BF), "x", 1)
    kept = lax.all_gather(dot(wide, own[2]).astype(BF), "c")
    kept, basis = tie((kept, basis))

    gram = mm("li,lj->ij", basis, out_basis).astype(BF)
    near = swap(gram, "za", 1)
    field = (dot(own[1], field) + dot(other[1], swap(field, "zb", 1))).astype(BF)
    field, came, kept = tie((field, came, kept))

    came = lax.all_gather(came, "c")
    tail = in_order([kept[:, :rank], came[:, :rank], kept[:, rank:], came[:, rank:]], "x")
    tail = tie(jnp.concatenate(tail, 1))

    field = lax.all_gather(field, "c")
    field, near = lax.optimization_barrier((field, near))
    chain = jnp.concatenate([dot(own[0], gram).astype(BF), dot(other[0], near).astype(BF)], 1)
    field = lax.dynamic_slice_in_dim(field, core * half, half, 2)
    share = add_up(tail, field)
    totals = hand_out(share, QUAD + LINE).reshape(4 * rank, half)

    chain_far = swap(chain, "zb", 1)
    mine = dot(own[1], chain).astype(BF)
    theirs = dot(other[1], chain_far).astype(BF)
    back = in_order([mine[:, :rank], mine[:, rank:], theirs[:, :rank], theirs[:, rank:]], QUAD)
    back = [lax.all_gather(jnp.concatenate(back[i : i + 2], 1), "c") for i in (0, 2)]
    back = jnp.concatenate(back, 2)

    field = (field.astype(F32) - mm("cij,jr->cir", back, totals)).astype(BF)
    share = add_up(tail, lax.optimization_barrier(field))
    total = hand_out(share, LINE).reshape(rank, half)
    return finish(rhs, out_basis, lax.all_gather(total, "c"))[None]


def solution(mesh):
    devices = mesh.devices.reshape(4, 2, 2, 2, 8, 2)
    fine = Mesh(devices, ("x", "zb", "za", "zl", "y", "c"))
    bfly, cols = ("x", "zb", "za"), ("zl", "y", "c")
    in_specs = (
        P(bfly, cols, None),
        P(bfly, cols, None),
        P(bfly, cols, None),
        P(None, bfly, cols, None, None, None),
    )
    out_specs = P(bfly, cols, None)
    return jax.shard_map(body, mesh=fine, in_specs=in_specs, out_specs=out_specs, check_vma=False)
```

```python
import jax
import jax.numpy as jnp
from jax import lax
from jax.experimental import pallas as pl
from jax.experimental.pallas import tpu as pltpu
from jax.sharding import Mesh, PartitionSpec as P

BF = jnp.bfloat16
F32 = jnp.float32
LINE = ("zl", "y")
GROUP = ("x",) + LINE
QUAD = ("zb", "za")
CHUNKS = 4


def swap(block, axis, bit):
    size = lax.axis_size(axis)
    return lax.ppermute(block, axis, [(i, i ^ bit) for i in range(size)])


def mm(spec, a, b):
    return jnp.einsum(spec, a, b, preferred_element_type=F32)


def dot(a, b):
    return jnp.dot(a, b, preferred_element_type=F32)


def in_order(blocks, axis):
    me = lax.axis_index(axis)
    for bit in (1, 2):
        turned = [blocks[d ^ bit] for d in range(len(blocks))]
        blocks = [jnp.where(me & bit == bit, t, b) for t, b in zip(turned, blocks)]
    return blocks


def add_up(tail, coefficient):
    spread = mm("cij,cjr->ir", tail, coefficient).astype(BF)
    pieces = spread.reshape(lax.axis_size(GROUP), -1, coefficient.shape[2])
    pieces = lax.all_to_all(pieces, GROUP, 0, 0, tiled=True)
    return jnp.sum(pieces.astype(F32), axis=0).astype(BF)


def hand_out(share, axes):
    copies = jnp.broadcast_to(share, (lax.axis_size(axes), *share.shape))
    return lax.all_to_all(copies, axes, 0, 0, tiled=True)


def finish_kernel(rhs_hbm, basis_hbm, total_hbm, out_hbm, rhs, basis, total, out, sems):
    rows = rhs.shape[0] // CHUNKS
    half = total.shape[2]
    first = pltpu.make_async_copy(total_hbm, total, sems.at[0, CHUNKS])
    first.start()
    loads = []
    for i in range(CHUNKS):
        part = pl.ds(i * rows, rows)
        loads.append(
            (
                pltpu.make_async_copy(basis_hbm.at[part], basis.at[part], sems.at[0, i]),
                pltpu.make_async_copy(rhs_hbm.at[part], rhs.at[part], sems.at[1, i]),
            )
        )
        for load in loads[-1]:
            load.start()
    first.wait()
    stores = []
    for i in range(CHUNKS):
        part = pl.ds(i * rows, rows)
        for load in loads[i]:
            load.wait()
        for core in range(2):
            cols = slice(core * half, (core + 1) * half)
            out[part, cols] = rhs[part, cols].astype(F32) - dot(basis[part], total[core])
        stores.append(pltpu.make_async_copy(out.at[part], out_hbm.at[part], sems.at[2, i]))
        stores[-1].start()
    for store in stores:
        store.wait()


def finish(rhs, basis, total):
    return pl.pallas_call(
        finish_kernel,
        in_specs=[pl.BlockSpec(memory_space=pl.ANY)] * 3,
        out_specs=pl.BlockSpec(memory_space=pl.ANY),
        out_shape=jax.ShapeDtypeStruct(rhs.shape, F32),
        scratch_shapes=[
            pltpu.VMEM(rhs.shape, BF),
            pltpu.VMEM(basis.shape, BF),
            pltpu.VMEM(total.shape, BF),
            pltpu.VMEM(rhs.shape, F32),
            pltpu.SemaphoreType.DMA((3, CHUNKS + 1)),
        ],
        compiler_params=pltpu.CompilerParams(vmem_limit_bytes=16 * 1024 * 1024),
    )(rhs, basis, total)


def body(right_side, column_leaf_factors, leaf_out, transfer):
    rhs, basis, out_basis = right_side[0], column_leaf_factors[0], leaf_out[0]
    half = rhs.shape[1] // 2
    rank = basis.shape[1]
    core = lax.axis_index("c")

    tie = lax.optimization_barrier
    parts = [mm("lk,lr->kr", basis, rhs[:, :half]).astype(BF)]
    parts[0], basis = tie((parts[0], basis))
    parts.append(mm("lk,lr->kr", basis, rhs[:, half:]).astype(BF))
    parts[1], transfer = tie((parts[1], transfer))
    own = transfer[:, 0, 0, 0]
    other = transfer[:, 0, 0, 1]

    far = swap(other[3], "x", 2)
    parts = [(dot(own[0], p) + dot(other[0], swap(p, "za", 1))).astype(BF) for p in parts]
    *_, far = tie((*parts, far))
    wide = jnp.concatenate([own[3], far], 0)
    came = swap(dot(wide, other[2]).astype(BF), "x", 1)
    kept = lax.all_gather(dot(wide, own[2]).astype(BF), "c")
    kept, basis = tie((kept, basis))

    gram = mm("li,lj->ij", basis, out_basis).astype(BF)
    near = swap(gram, "za", 1)
    parts = [(dot(own[1], p) + dot(other[1], swap(p, "zb", 1))).astype(BF) for p in parts]
    *_, came, kept = tie((*parts, came, kept))

    came = lax.all_gather(came, "c")
    tail = in_order([kept[:, :rank], came[:, :rank], kept[:, rank:], came[:, rank:]], "x")
    tail = tie(jnp.concatenate(tail, 1))

    parts = [lax.all_gather(p, "c") for p in parts]
    field = jnp.where(core == 0, parts[0], parts[1])
    field, near = lax.optimization_barrier((field, near))
    chain = jnp.concatenate([dot(own[0], gram).astype(BF), dot(other[0], near).astype(BF)], 1)
    share = add_up(tail, field)
    totals = hand_out(share, QUAD + LINE).reshape(4 * rank, half)

    chain_far = swap(chain, "zb", 1)
    mine = dot(own[1], chain).astype(BF)
    theirs = dot(other[1], chain_far).astype(BF)
    back = in_order([mine[:, :rank], mine[:, rank:], theirs[:, :rank], theirs[:, rank:]], QUAD)
    back = [lax.all_gather(jnp.concatenate(back[i : i + 2], 1), "c") for i in (0, 2)]
    back = jnp.concatenate(back, 2)

    field = (field.astype(F32) - mm("cij,jr->cir", back, totals)).astype(BF)
    share = add_up(tail, lax.optimization_barrier(field))
    total = hand_out(share, LINE).reshape(rank, half)
    return finish(rhs, out_basis, lax.all_gather(total, "c"))[None]


def solution(mesh):
    devices = mesh.devices.reshape(4, 2, 2, 2, 8, 2)
    fine = Mesh(devices, ("x", "zb", "za", "zl", "y", "c"))
    bfly, cols = ("x", "zb", "za"), ("zl", "y", "c")
    in_specs = (
        P(bfly, cols, None),
        P(bfly, cols, None),
        P(bfly, cols, None),
        P(None, bfly, cols, None, None, None),
    )
    out_specs = P(bfly, cols, None)
    return jax.shard_map(body, mesh=fine, in_specs=in_specs, out_specs=out_specs, check_vma=False)
```

```python
import jax
import jax.numpy as jnp
from jax import lax
from jax.experimental import pallas as pl
from jax.experimental.pallas import tpu as pltpu
from jax.sharding import Mesh, PartitionSpec as P

BF = jnp.bfloat16
F32 = jnp.float32
LINE = ("zl", "y")
GROUP = ("x",) + LINE
QUAD = ("zb", "za")
CHUNKS = 4


def swap(block, axis, bit):
    size = lax.axis_size(axis)
    return lax.ppermute(block, axis, [(i, i ^ bit) for i in range(size)])


def mm(spec, a, b):
    return jnp.einsum(spec, a, b, preferred_element_type=F32)


def dot(a, b):
    return jnp.dot(a, b, preferred_element_type=F32)


def in_order(blocks, axis):
    me = lax.axis_index(axis)
    for bit in (1, 2):
        turned = [blocks[d ^ bit] for d in range(len(blocks))]
        blocks = [jnp.where(me & bit == bit, t, b) for t, b in zip(turned, blocks)]
    return blocks


def add_up(tail, coefficient):
    spread = mm("cij,cjr->ir", tail, coefficient).astype(BF)
    pieces = spread.reshape(lax.axis_size(GROUP), -1, coefficient.shape[2])
    pieces = lax.all_to_all(pieces, GROUP, 0, 0, tiled=True)
    return jnp.sum(pieces.astype(F32), axis=0).astype(BF)


def add_over(share, axes):
    pieces = share.reshape(lax.axis_size(axes), -1, share.shape[1])
    pieces = lax.all_to_all(pieces, axes, 0, 0, tiled=True)
    return jnp.sum(pieces.astype(F32), axis=0).astype(BF)


def hand_out(share, axes):
    copies = jnp.broadcast_to(share, (lax.axis_size(axes), *share.shape))
    return lax.all_to_all(copies, axes, 0, 0, tiled=True)


def finish_kernel(rhs_hbm, basis_hbm, total_hbm, out_hbm, rhs, basis, total, out, sems):
    rows = rhs.shape[0] // CHUNKS
    half = total.shape[2]
    first = pltpu.make_async_copy(total_hbm, total, sems.at[0, CHUNKS])
    first.start()
    loads = []
    for i in range(CHUNKS):
        part = pl.ds(i * rows, rows)
        loads.append(
            (
                pltpu.make_async_copy(basis_hbm.at[part], basis.at[part], sems.at[0, i]),
                pltpu.make_async_copy(rhs_hbm.at[part], rhs.at[part], sems.at[1, i]),
            )
        )
        for load in loads[-1]:
            load.start()
    first.wait()
    stores = []
    for i in range(CHUNKS):
        part = pl.ds(i * rows, rows)
        for load in loads[i]:
            load.wait()
        for core in range(2):
            cols = slice(core * half, (core + 1) * half)
            out[part, cols] = rhs[part, cols].astype(F32) - dot(basis[part], total[core])
        stores.append(pltpu.make_async_copy(out.at[part], out_hbm.at[part], sems.at[2, i]))
        stores[-1].start()
    for store in stores:
        store.wait()


def finish(rhs, basis, total):
    return pl.pallas_call(
        finish_kernel,
        in_specs=[pl.BlockSpec(memory_space=pl.ANY)] * 3,
        out_specs=pl.BlockSpec(memory_space=pl.ANY),
        out_shape=jax.ShapeDtypeStruct(rhs.shape, F32),
        scratch_shapes=[
            pltpu.VMEM(rhs.shape, BF),
            pltpu.VMEM(basis.shape, BF),
            pltpu.VMEM(total.shape, BF),
            pltpu.VMEM(rhs.shape, F32),
            pltpu.SemaphoreType.DMA((3, CHUNKS + 1)),
        ],
        compiler_params=pltpu.CompilerParams(vmem_limit_bytes=16 * 1024 * 1024),
    )(rhs, basis, total)


def body(right_side, column_leaf_factors, leaf_out, transfer):
    rhs, basis, out_basis = right_side[0], column_leaf_factors[0], leaf_out[0]
    half = rhs.shape[1] // 2
    rank = basis.shape[1]
    core = lax.axis_index("c")

    tie = lax.optimization_barrier
    start = mm("lk,lr->kr", basis, rhs).astype(BF)
    start, transfer = tie((start, transfer))
    own = transfer[:, 0, 0, 0]
    other = transfer[:, 0, 0, 1]

    far = swap(other[3], "x", 2)
    field = (dot(own[0], start) + dot(other[0], swap(start, "za", 1))).astype(BF)
    field, far = tie((field, far))
    wide = jnp.concatenate([own[3], far], 0)
    came = swap(dot(wide, other[2]).astype(BF), "x", 1)
    kept = lax.all_gather(dot(wide, own[2]).astype(BF), "c")
    kept, basis = tie((kept, basis))

    gram = mm("li,lj->ij", basis, out_basis).astype(BF)
    near = swap(gram, "za", 1)
    field = (dot(own[1], field) + dot(other[1], swap(field, "zb", 1))).astype(BF)
    field, came, kept = tie((field, came, kept))

    keep = lax.dynamic_slice_in_dim(field, core * half, half, 1)
    give = lax.dynamic_slice_in_dim(field, (1 - core) * half, half, 1)
    both = lax.all_gather(jnp.concatenate([came, give], 0), "c")
    came = both[:, : 2 * rank]
    field = jnp.where(lax.broadcasted_iota(jnp.int32, (2, 1, 1), 0) == core, keep, both[:, 2 * rank :])
    tail = in_order([kept[:, :rank], came[:, :rank], kept[:, rank:], came[:, rank:]], "x")
    tail = tie(jnp.concatenate(tail, 1))

    field, near = lax.optimization_barrier((field, near))
    chain = jnp.concatenate([dot(own[0], gram).astype(BF), dot(other[0], near).astype(BF)], 1)
    share = add_over(mm("cij,cjr->ir", tail, field).astype(BF), "x")
    share, chain = tie((share, chain))
    chain_far = swap(chain, "zb", 1)
    share = add_over(share, LINE)
    totals = hand_out(share, QUAD + LINE).reshape(4 * rank, half)

    mine = dot(own[1], chain).astype(BF)
    theirs = dot(other[1], chain_far).astype(BF)
    back = in_order([mine[:, :rank], mine[:, rank:], theirs[:, :rank], theirs[:, rank:]], QUAD)
    back = [lax.all_gather(jnp.concatenate(back[i : i + 2], 1), "c") for i in (0, 2)]
    back = jnp.concatenate(back, 2)

    field = (field.astype(F32) - mm("cij,jr->cir", back, totals)).astype(BF)
    share = add_up(tail, lax.optimization_barrier(field))
    total = hand_out(share, LINE).reshape(rank, half)
    return finish(rhs, out_basis, lax.all_gather(total, "c"))[None]


def solution(mesh):
    devices = mesh.devices.reshape(4, 2, 2, 2, 8, 2)
    fine = Mesh(devices, ("x", "zb", "za", "zl", "y", "c"))
    bfly, cols = ("x", "zb", "za"), ("zl", "y", "c")
    in_specs = (
        P(bfly, cols, None),
        P(bfly, cols, None),
        P(bfly, cols, None),
        P(None, bfly, cols, None, None, None),
    )
    out_specs = P(bfly, cols, None)
    return jax.shard_map(body, mesh=fine, in_specs=in_specs, out_specs=out_specs, check_vma=False)
```

```python
import jax
import jax.numpy as jnp
from jax import lax
from jax.experimental import pallas as pl
from jax.experimental.pallas import tpu as pltpu
from jax.sharding import Mesh, PartitionSpec as P

BF = jnp.bfloat16
F32 = jnp.float32
LINE = ("zl", "y")
GROUP = ("x",) + LINE
QUAD = ("zb", "za")
CHUNKS = 4


def swap(block, axis, bit):
    size = lax.axis_size(axis)
    return lax.ppermute(block, axis, [(i, i ^ bit) for i in range(size)])


def mm(spec, a, b):
    return jnp.einsum(spec, a, b, preferred_element_type=F32)


def dot(a, b):
    return jnp.dot(a, b, preferred_element_type=F32)


def in_order(blocks, axis):
    me = lax.axis_index(axis)
    for bit in (1, 2):
        turned = [blocks[d ^ bit] for d in range(len(blocks))]
        blocks = [jnp.where(me & bit == bit, t, b) for t, b in zip(turned, blocks)]
    return blocks


def add_up(tail, coefficient):
    spread = mm("cij,cjr->ir", tail, coefficient).astype(BF)
    pieces = spread.reshape(lax.axis_size(GROUP), -1, coefficient.shape[2])
    pieces = lax.all_to_all(pieces, GROUP, 0, 0, tiled=True)
    return jnp.sum(pieces.astype(F32), axis=0).astype(BF)


def hand_out(share, axes):
    copies = jnp.broadcast_to(share, (lax.axis_size(axes), *share.shape))
    return lax.all_to_all(copies, axes, 0, 0, tiled=True)


def finish_kernel(rhs_hbm, basis_hbm, total_hbm, out_hbm, rhs, basis, total, out, sems):
    rows = rhs.shape[0] // CHUNKS
    half = total.shape[2]
    first = pltpu.make_async_copy(total_hbm, total, sems.at[0, CHUNKS])
    first.start()
    loads = []
    for i in range(CHUNKS):
        part = pl.ds(i * rows, rows)
        loads.append(
            (
                pltpu.make_async_copy(basis_hbm.at[part], basis.at[part], sems.at[0, i]),
                pltpu.make_async_copy(rhs_hbm.at[part], rhs.at[part], sems.at[1, i]),
            )
        )
        for load in loads[-1]:
            load.start()
    first.wait()
    stores = []
    for i in range(CHUNKS):
        part = pl.ds(i * rows, rows)
        for load in loads[i]:
            load.wait()
        for core in range(2):
            cols = slice(core * half, (core + 1) * half)
            out[part, cols] = rhs[part, cols].astype(F32) - dot(basis[part], total[core])
        stores.append(pltpu.make_async_copy(out.at[part], out_hbm.at[part], sems.at[2, i]))
        stores[-1].start()
    for store in stores:
        store.wait()


def finish(rhs, basis, total):
    return pl.pallas_call(
        finish_kernel,
        in_specs=[pl.BlockSpec(memory_space=pl.ANY)] * 3,
        out_specs=pl.BlockSpec(memory_space=pl.ANY),
        out_shape=jax.ShapeDtypeStruct(rhs.shape, F32),
        scratch_shapes=[
            pltpu.VMEM(rhs.shape, BF),
            pltpu.VMEM(basis.shape, BF),
            pltpu.VMEM(total.shape, BF),
            pltpu.VMEM(rhs.shape, F32),
            pltpu.SemaphoreType.DMA((3, CHUNKS + 1)),
        ],
        compiler_params=pltpu.CompilerParams(vmem_limit_bytes=16 * 1024 * 1024),
    )(rhs, basis, total)


def body(right_side, column_leaf_factors, leaf_out, transfer):
    rhs, basis, out_basis = right_side[0], column_leaf_factors[0], leaf_out[0]
    half = rhs.shape[1] // 2
    rank = basis.shape[1]
    core = lax.axis_index("c")

    tie = lax.optimization_barrier
    start = mm("lk,lr->kr", basis, rhs).astype(BF)
    start, transfer = tie((start, transfer))
    own = transfer[:, 0, 0, 0]
    other = transfer[:, 0, 0, 1]

    far = swap(other[3], "x", 2)
    field = (dot(own[0], start) + dot(other[0], swap(start, "za", 1))).astype(BF)
    field, far = tie((field, far))
    wide = jnp.concatenate([own[3], far], 0)
    came = swap(dot(wide, other[2]).astype(BF), "x", 1)
    kept = lax.all_gather(dot(wide, own[2]).astype(BF), "c")
    kept, basis = tie((kept, basis))

    gram = mm("li,lj->ij", basis, out_basis).astype(BF)
    near = swap(gram, "za", 1)
    field = (dot(own[1], field) + dot(other[1], swap(field, "zb", 1))).astype(BF)
    field, came, kept = tie((field, came, kept))

    keep = lax.dynamic_slice_in_dim(field, core * half, half, 1)
    give = lax.dynamic_slice_in_dim(field, (1 - core) * half, half, 1)
    both = lax.all_gather(jnp.concatenate([came, give], 0), "c")
    came = both[:, : 2 * rank]
    field = jnp.where(lax.broadcasted_iota(jnp.int32, (2, 1, 1), 0) == core, keep, both[:, 2 * rank :])
    tail = in_order([kept[:, :rank], came[:, :rank], kept[:, rank:], came[:, rank:]], "x")
    tail = tie(jnp.concatenate(tail, 1))

    field, near = lax.optimization_barrier((field, near))
    chain = jnp.concatenate([dot(own[0], gram).astype(BF), dot(other[0], near).astype(BF)], 1)
    field = tie(field)
    share = add_up(tail, field)
    totals = hand_out(share, QUAD + LINE).reshape(4 * rank, half)

    chain_far = swap(chain, "zb", 1)
    mine = dot(own[1], chain).astype(BF)
    theirs = dot(other[1], chain_far).astype(BF)
    back = in_order([mine[:, :rank], mine[:, rank:], theirs[:, :rank], theirs[:, rank:]], QUAD)
    back = [lax.all_gather(jnp.concatenate(back[i : i + 2], 1), "c") for i in (0, 2)]
    back = jnp.concatenate(back, 2)

    field = (field.astype(F32) - mm("cij,jr->cir", back, totals)).astype(BF)
    share = add_up(tail, lax.optimization_barrier(field))
    total = hand_out(share, LINE).reshape(rank, half)
    return finish(rhs, out_basis, lax.all_gather(total, "c"))[None]


def solution(mesh):
    devices = mesh.devices.reshape(4, 2, 2, 2, 8, 2)
    fine = Mesh(devices, ("x", "zb", "za", "zl", "y", "c"))
    bfly, cols = ("x", "zb", "za"), ("zl", "y", "c")
    in_specs = (
        P(bfly, cols, None),
        P(bfly, cols, None),
        P(bfly, cols, None),
        P(None, bfly, cols, None, None, None),
    )
    out_specs = P(bfly, cols, None)
    return jax.shard_map(body, mesh=fine, in_specs=in_specs, out_specs=out_specs, check_vma=False)
```

```python
import jax
import jax.numpy as jnp
from jax import lax
from jax.experimental import pallas as pl
from jax.experimental.pallas import tpu as pltpu
from jax.sharding import Mesh, PartitionSpec as P

BF = jnp.bfloat16
F32 = jnp.float32
LINE = ("zl", "y")
GROUP = ("x",) + LINE
QUAD = ("zb", "za")
CHUNKS = 4


def swap(block, axis, bit):
    size = lax.axis_size(axis)
    return lax.ppermute(block, axis, [(i, i ^ bit) for i in range(size)])


def mm(spec, a, b):
    return jnp.einsum(spec, a, b, preferred_element_type=F32)


def dot(a, b):
    return jnp.dot(a, b, preferred_element_type=F32)


def in_order(blocks, axis):
    me = lax.axis_index(axis)
    for bit in (1, 2):
        turned = [blocks[d ^ bit] for d in range(len(blocks))]
        blocks = [jnp.where(me & bit == bit, t, b) for t, b in zip(turned, blocks)]
    return blocks


def add_up(spread):
    pieces = spread.reshape(lax.axis_size(GROUP), -1, spread.shape[1])
    pieces = lax.all_to_all(pieces, GROUP, 0, 0, tiled=True)
    return jnp.sum(pieces.astype(F32), axis=0).astype(BF)


def hand_out(share, axes):
    copies = jnp.broadcast_to(share, (lax.axis_size(axes), *share.shape))
    return lax.all_to_all(copies, axes, 0, 0, tiled=True)


def finish_kernel(rhs_hbm, basis_hbm, total_hbm, out_hbm, rhs, basis, total, out, sems):
    rows = rhs.shape[0] // CHUNKS
    half = total.shape[2]
    first = pltpu.make_async_copy(total_hbm, total, sems.at[0, CHUNKS])
    first.start()
    loads = []
    for i in range(CHUNKS):
        part = pl.ds(i * rows, rows)
        loads.append(
            (
                pltpu.make_async_copy(basis_hbm.at[part], basis.at[part], sems.at[0, i]),
                pltpu.make_async_copy(rhs_hbm.at[part], rhs.at[part], sems.at[1, i]),
            )
        )
        for load in loads[-1]:
            load.start()
    first.wait()
    stores = []
    for i in range(CHUNKS):
        part = pl.ds(i * rows, rows)
        for load in loads[i]:
            load.wait()
        for core in range(2):
            cols = slice(core * half, (core + 1) * half)
            out[part, cols] = rhs[part, cols].astype(F32) - dot(basis[part], total[core])
        stores.append(pltpu.make_async_copy(out.at[part], out_hbm.at[part], sems.at[2, i]))
        stores[-1].start()
    for store in stores:
        store.wait()


def finish(rhs, basis, total):
    return pl.pallas_call(
        finish_kernel,
        in_specs=[pl.BlockSpec(memory_space=pl.ANY)] * 3,
        out_specs=pl.BlockSpec(memory_space=pl.ANY),
        out_shape=jax.ShapeDtypeStruct(rhs.shape, F32),
        scratch_shapes=[
            pltpu.VMEM(rhs.shape, BF),
            pltpu.VMEM(basis.shape, BF),
            pltpu.VMEM(total.shape, BF),
            pltpu.VMEM(rhs.shape, F32),
            pltpu.SemaphoreType.DMA((3, CHUNKS + 1)),
        ],
        compiler_params=pltpu.CompilerParams(vmem_limit_bytes=16 * 1024 * 1024),
    )(rhs, basis, total)


def body(right_side, column_leaf_factors, leaf_out, transfer):
    rhs, basis, out_basis = right_side[0], column_leaf_factors[0], leaf_out[0]
    half = rhs.shape[1] // 2
    rank = basis.shape[1]
    core = lax.axis_index("c")

    tie = lax.optimization_barrier
    start = mm("lk,lr->kr", basis, rhs).astype(BF)
    start, transfer = tie((start, transfer))
    own = transfer[:, 0, 0, 0]
    other = transfer[:, 0, 0, 1]

    far = swap(other[3], "x", 2)
    field = (dot(own[0], start) + dot(other[0], swap(start, "za", 1))).astype(BF)
    field, far = tie((field, far))
    wide = jnp.concatenate([own[3], far], 0)
    came = swap(dot(wide, other[2]).astype(BF), "x", 1)
    kept = lax.all_gather(dot(wide, own[2]).astype(BF), "c")
    kept, basis = tie((kept, basis))

    gram = mm("li,lj->ij", basis, out_basis).astype(BF)
    near = swap(gram, "za", 1)
    field = (dot(own[1], field) + dot(other[1], swap(field, "zb", 1))).astype(BF)
    field, came, kept = tie((field, came, kept))

    keep = lax.dynamic_slice_in_dim(field, core * half, half, 1)
    give = lax.dynamic_slice_in_dim(field, (1 - core) * half, half, 1)
    both = lax.all_gather(jnp.concatenate([came, give], 0), "c")
    came = both[:, : 2 * rank]
    field = jnp.where(lax.broadcasted_iota(jnp.int32, (2, 1, 1), 0) == core, keep, both[:, 2 * rank :])
    tail = in_order([kept[:, :rank], came[:, :rank], kept[:, rank:], came[:, rank:]], "x")
    tail = tie(jnp.concatenate(tail, 1))

    field, near = lax.optimization_barrier((field, near))
    chain = jnp.concatenate([dot(own[0], gram).astype(BF), dot(other[0], near).astype(BF)], 1)
    field = tie(field)
    spread = mm("cij,cjr->ir", tail, field).astype(BF)
    share = add_up(spread)
    totals = hand_out(share, QUAD + LINE).reshape(4 * rank, half)

    chain_far = swap(chain, "zb", 1)
    mine = dot(own[1], chain).astype(BF)
    theirs = dot(other[1], chain_far).astype(BF)
    back = in_order([mine[:, :rank], mine[:, rank:], theirs[:, :rank], theirs[:, rank:]], QUAD)
    back = [lax.all_gather(jnp.concatenate(back[i : i + 2], 1), "c") for i in (0, 2)]
    back = jnp.concatenate(back, 2)

    whole, spread = tie((mm("cij,cjk->ik", tail, back).astype(BF), spread))
    spread = (spread.astype(F32) - dot(whole, totals)).astype(BF)
    share = add_up(spread)
    total = hand_out(share, LINE).reshape(rank, half)
    return finish(rhs, out_basis, lax.all_gather(total, "c"))[None]


def solution(mesh):
    devices = mesh.devices.reshape(4, 2, 2, 2, 8, 2)
    fine = Mesh(devices, ("x", "zb", "za", "zl", "y", "c"))
    bfly, cols = ("x", "zb", "za"), ("zl", "y", "c")
    in_specs = (
        P(bfly, cols, None),
        P(bfly, cols, None),
        P(bfly, cols, None),
        P(None, bfly, cols, None, None, None),
    )
    out_specs = P(bfly, cols, None)
    return jax.shard_map(body, mesh=fine, in_specs=in_specs, out_specs=out_specs, check_vma=False)
```

```python
import jax
import jax.numpy as jnp
from jax import lax
from jax.experimental import pallas as pl
from jax.experimental.pallas import tpu as pltpu
from jax.sharding import Mesh, PartitionSpec as P

BF = jnp.bfloat16
F32 = jnp.float32
LINE = ("zl", "y")
GROUP = ("x",) + LINE
QUAD = ("zb", "za")
CHUNKS = 4


def swap(block, axis, bit):
    size = lax.axis_size(axis)
    return lax.ppermute(block, axis, [(i, i ^ bit) for i in range(size)])


def mm(spec, a, b):
    return jnp.einsum(spec, a, b, preferred_element_type=F32)


def dot(a, b):
    return jnp.dot(a, b, preferred_element_type=F32)


def in_order(blocks, axis):
    me = lax.axis_index(axis)
    for bit in (1, 2):
        turned = [blocks[d ^ bit] for d in range(len(blocks))]
        blocks = [jnp.where(me & bit == bit, t, b) for t, b in zip(turned, blocks)]
    return blocks


def add_up(tail, coefficient):
    spread = mm("cij,cjr->ir", tail, coefficient).astype(BF)
    pieces = spread.reshape(lax.axis_size(GROUP), -1, coefficient.shape[2])
    pieces = lax.all_to_all(pieces, GROUP, 0, 0, tiled=True)
    return jnp.sum(pieces.astype(F32), axis=0).astype(BF)


def add_over(share, axes):
    pieces = share.reshape(lax.axis_size(axes), -1, share.shape[1])
    pieces = lax.all_to_all(pieces, axes, 0, 0, tiled=True)
    return jnp.sum(pieces.astype(F32), axis=0).astype(BF)


def hand_out(share, axes):
    copies = jnp.broadcast_to(share, (lax.axis_size(axes), *share.shape))
    return lax.all_to_all(copies, axes, 0, 0, tiled=True)


def finish_kernel(rhs_hbm, basis_hbm, total_hbm, out_hbm, rhs, basis, total, out, sems):
    rows = rhs.shape[0] // CHUNKS
    half = total.shape[2]
    first = pltpu.make_async_copy(total_hbm, total, sems.at[0, CHUNKS])
    first.start()
    loads = []
    for i in range(CHUNKS):
        part = pl.ds(i * rows, rows)
        loads.append(
            (
                pltpu.make_async_copy(basis_hbm.at[part], basis.at[part], sems.at[0, i]),
                pltpu.make_async_copy(rhs_hbm.at[part], rhs.at[part], sems.at[1, i]),
            )
        )
        for load in loads[-1]:
            load.start()
    first.wait()
    stores = []
    for i in range(CHUNKS):
        part = pl.ds(i * rows, rows)
        for load in loads[i]:
            load.wait()
        for core in range(2):
            cols = slice(core * half, (core + 1) * half)
            out[part, cols] = rhs[part, cols].astype(F32) - dot(basis[part], total[core])
        stores.append(pltpu.make_async_copy(out.at[part], out_hbm.at[part], sems.at[2, i]))
        stores[-1].start()
    for store in stores:
        store.wait()


def finish(rhs, basis, total):
    return pl.pallas_call(
        finish_kernel,
        in_specs=[pl.BlockSpec(memory_space=pl.ANY)] * 3,
        out_specs=pl.BlockSpec(memory_space=pl.ANY),
        out_shape=jax.ShapeDtypeStruct(rhs.shape, F32),
        scratch_shapes=[
            pltpu.VMEM(rhs.shape, BF),
            pltpu.VMEM(basis.shape, BF),
            pltpu.VMEM(total.shape, BF),
            pltpu.VMEM(rhs.shape, F32),
            pltpu.SemaphoreType.DMA((3, CHUNKS + 1)),
        ],
        compiler_params=pltpu.CompilerParams(vmem_limit_bytes=16 * 1024 * 1024),
    )(rhs, basis, total)


def body(right_side, column_leaf_factors, leaf_out, transfer):
    rhs, basis, out_basis = right_side[0], column_leaf_factors[0], leaf_out[0]
    half = rhs.shape[1] // 2
    rank = basis.shape[1]
    core = lax.axis_index("c")

    tie = lax.optimization_barrier
    start = mm("lk,lr->kr", basis, rhs).astype(BF)
    start, transfer = tie((start, transfer))
    own = transfer[:, 0, 0, 0]
    other = transfer[:, 0, 0, 1]

    far = swap(other[3], "x", 2)
    field = (dot(own[0], start) + dot(other[0], swap(start, "za", 1))).astype(BF)
    field, far = tie((field, far))
    wide = jnp.concatenate([own[3], far], 0)
    came = swap(dot(wide, other[2]).astype(BF), "x", 1)
    kept = lax.all_gather(dot(wide, own[2]).astype(BF), "c")
    kept, basis = tie((kept, basis))

    gram = mm("li,lj->ij", basis, out_basis).astype(BF)
    near = swap(gram, "za", 1)
    field = (dot(own[1], field) + dot(other[1], swap(field, "zb", 1))).astype(BF)
    field, came, kept = tie((field, came, kept))

    keep = lax.dynamic_slice_in_dim(field, core * half, half, 1)
    give = lax.dynamic_slice_in_dim(field, (1 - core) * half, half, 1)
    both = lax.all_gather(jnp.concatenate([came, give], 0), "c")
    came = both[:, : 2 * rank]
    field = jnp.where(lax.broadcasted_iota(jnp.int32, (2, 1, 1), 0) == core, keep, both[:, 2 * rank :])
    tail = in_order([kept[:, :rank], came[:, :rank], kept[:, rank:], came[:, rank:]], "x")
    tail = tie(jnp.concatenate(tail, 1))

    field, near = lax.optimization_barrier((field, near))
    chain = jnp.concatenate([dot(own[0], gram).astype(BF), dot(other[0], near).astype(BF)], 1)
    share = add_over(mm("cij,cjr->ir", tail, field).astype(BF), "x")
    chain_far = swap(chain, "zb", 1)
    share, chain_far = tie((add_over(share, LINE), chain_far))
    totals = hand_out(share, QUAD + LINE).reshape(4 * rank, half)

    mine = dot(own[1], chain).astype(BF)
    theirs = dot(other[1], chain_far).astype(BF)
    back = in_order([mine[:, :rank], mine[:, rank:], theirs[:, :rank], theirs[:, rank:]], QUAD)
    back = [lax.all_gather(jnp.concatenate(back[i : i + 2], 1), "c") for i in (0, 2)]
    back = jnp.concatenate(back, 2)

    field = (field.astype(F32) - mm("cij,jr->cir", back, totals)).astype(BF)
    share = add_up(tail, lax.optimization_barrier(field))
    total = hand_out(share, LINE).reshape(rank, half)
    return finish(rhs, out_basis, lax.all_gather(total, "c"))[None]


def solution(mesh):
    devices = mesh.devices.reshape(4, 2, 2, 2, 8, 2)
    fine = Mesh(devices, ("x", "zb", "za", "zl", "y", "c"))
    bfly, cols = ("x", "zb", "za"), ("zl", "y", "c")
    in_specs = (
        P(bfly, cols, None),
        P(bfly, cols, None),
        P(bfly, cols, None),
        P(None, bfly, cols, None, None, None),
    )
    out_specs = P(bfly, cols, None)
    return jax.shard_map(body, mesh=fine, in_specs=in_specs, out_specs=out_specs, check_vma=False)
```

```python
import jax
import jax.numpy as jnp
from jax import lax
from jax.experimental import pallas as pl
from jax.experimental.pallas import tpu as pltpu
from jax.sharding import Mesh, PartitionSpec as P

BF = jnp.bfloat16
F32 = jnp.float32
LINE = ("zl", "y")
GROUP = ("x",) + LINE
QUAD = ("zb", "za")
CHUNKS = 8


def swap(block, axis, bit):
    size = lax.axis_size(axis)
    return lax.ppermute(block, axis, [(i, i ^ bit) for i in range(size)])


def mm(spec, a, b):
    return jnp.einsum(spec, a, b, preferred_element_type=F32)


def dot(a, b):
    return jnp.dot(a, b, preferred_element_type=F32)


def in_order(blocks, axis):
    me = lax.axis_index(axis)
    for bit in (1, 2):
        turned = [blocks[d ^ bit] for d in range(len(blocks))]
        blocks = [jnp.where(me & bit == bit, t, b) for t, b in zip(turned, blocks)]
    return blocks


def add_up(tail, coefficient):
    spread = mm("cij,cjr->ir", tail, coefficient).astype(BF)
    pieces = spread.reshape(lax.axis_size(GROUP), -1, coefficient.shape[2])
    pieces = lax.all_to_all(pieces, GROUP, 0, 0, tiled=True)
    return jnp.sum(pieces.astype(F32), axis=0).astype(BF)


def hand_out(share, axes):
    copies = jnp.broadcast_to(share, (lax.axis_size(axes), *share.shape))
    return lax.all_to_all(copies, axes, 0, 0, tiled=True)


def finish_kernel(rhs_hbm, basis_hbm, total_hbm, out_hbm, rhs, basis, total, out, sems):
    rows = rhs.shape[0] // CHUNKS
    half = total.shape[2]
    first = pltpu.make_async_copy(total_hbm, total, sems.at[0, CHUNKS])
    first.start()
    loads = []
    for i in range(CHUNKS):
        part = pl.ds(i * rows, rows)
        loads.append(
            (
                pltpu.make_async_copy(basis_hbm.at[part], basis.at[part], sems.at[0, i]),
                pltpu.make_async_copy(rhs_hbm.at[part], rhs.at[part], sems.at[1, i]),
            )
        )
        for load in loads[-1]:
            load.start()
    first.wait()
    stores = []
    for i in range(CHUNKS):
        part = pl.ds(i * rows, rows)
        for load in loads[i]:
            load.wait()
        for core in range(2):
            cols = slice(core * half, (core + 1) * half)
            out[part, cols] = rhs[part, cols].astype(F32) - dot(basis[part], total[core])
        stores.append(pltpu.make_async_copy(out.at[part], out_hbm.at[part], sems.at[2, i]))
        stores[-1].start()
    for store in stores:
        store.wait()


def finish(rhs, basis, total):
    return pl.pallas_call(
        finish_kernel,
        in_specs=[pl.BlockSpec(memory_space=pl.ANY)] * 3,
        out_specs=pl.BlockSpec(memory_space=pl.ANY),
        out_shape=jax.ShapeDtypeStruct(rhs.shape, F32),
        scratch_shapes=[
            pltpu.VMEM(rhs.shape, BF),
            pltpu.VMEM(basis.shape, BF),
            pltpu.VMEM(total.shape, BF),
            pltpu.VMEM(rhs.shape, F32),
            pltpu.SemaphoreType.DMA((3, CHUNKS + 1)),
        ],
        compiler_params=pltpu.CompilerParams(vmem_limit_bytes=16 * 1024 * 1024),
    )(rhs, basis, total)


def body(right_side, column_leaf_factors, leaf_out, transfer):
    rhs, basis, out_basis = right_side[0], column_leaf_factors[0], leaf_out[0]
    half = rhs.shape[1] // 2
    rank = basis.shape[1]
    core = lax.axis_index("c")

    tie = lax.optimization_barrier
    start = mm("lk,lr->kr", basis, rhs).astype(BF)
    start, transfer = tie((start, transfer))
    own = transfer[:, 0, 0, 0]
    other = transfer[:, 0, 0, 1]

    far = swap(other[3], "x", 2)
    field = (dot(own[0], start) + dot(other[0], swap(start, "za", 1))).astype(BF)
    _, far = tie((field, far))
    wide = jnp.concatenate([own[3], far], 0)
    came = swap(dot(wide, other[2]).astype(BF), "x", 1)
    kept = lax.all_gather(dot(wide, own[2]).astype(BF), "c")
    kept, basis = tie((kept, basis))

    gram = mm("li,lj->ij", basis, out_basis).astype(BF)
    near = swap(gram, "za", 1)
    field = (dot(own[1], field) + dot(other[1], swap(field, "zb", 1))).astype(BF)
    _, came, kept = tie((field, came, kept))

    keep = lax.dynamic_slice_in_dim(field, core * half, half, 1)
    give = lax.dynamic_slice_in_dim(field, (1 - core) * half, half, 1)
    both = lax.all_gather(jnp.concatenate([came, give], 0), "c")
    came = both[:, : 2 * rank]
    field = jnp.where(lax.broadcasted_iota(jnp.int32, (2, 1, 1), 0) == core, keep, both[:, 2 * rank :])
    tail = in_order([kept[:, :rank], came[:, :rank], kept[:, rank:], came[:, rank:]], "x")
    tail = tie(jnp.concatenate(tail, 1))

    field, near = lax.optimization_barrier((field, near))
    chain = jnp.concatenate([dot(own[0], gram).astype(BF), dot(other[0], near).astype(BF)], 1)
    field = tie(field)
    share = add_up(tail, field)
    totals = hand_out(share, QUAD + LINE).reshape(4 * rank, half)

    chain_far = swap(chain, "zb", 1)
    mine = dot(own[1], chain).astype(BF)
    theirs = dot(other[1], chain_far).astype(BF)
    back = in_order([mine[:, :rank], mine[:, rank:], theirs[:, :rank], theirs[:, rank:]], QUAD)
    back = [lax.all_gather(jnp.concatenate(back[i : i + 2], 1), "c") for i in (0, 2)]
    back = jnp.concatenate(back, 2)

    field = (field.astype(F32) - mm("cij,jr->cir", back, totals)).astype(BF)
    share = add_up(tail, lax.optimization_barrier(field))
    total = hand_out(share, LINE).reshape(rank, half)
    return finish(rhs, out_basis, lax.all_gather(total, "c"))[None]


def solution(mesh):
    devices = mesh.devices.reshape(4, 2, 2, 2, 8, 2)
    fine = Mesh(devices, ("x", "zb", "za", "zl", "y", "c"))
    bfly, cols = ("x", "zb", "za"), ("zl", "y", "c")
    in_specs = (
        P(bfly, cols, None),
        P(bfly, cols, None),
        P(bfly, cols, None),
        P(None, bfly, cols, None, None, None),
    )
    out_specs = P(bfly, cols, None)
    return jax.shard_map(body, mesh=fine, in_specs=in_specs, out_specs=out_specs, check_vma=False)
```
